32 devices in a mesh: grp: 4 (over z), tp: 8 (over y, x, core).
Axes of the slice: x: 2, y: 2, z: 4, core: 2. Of those that a mesh axis runs over, the one named last changes fastest.
Arguments:
- tokens: bfloat16 [2048, 4096], P('grp', 'tp'), may hold values from -6 to 6
- token_tenant: int32 [2048], P('grp'), may hold values from 0 to 63, as said below
- tenant_storage_slot: int32 [64], replicated, may hold values from 0 to 63, as said below
- gate_matrix: bfloat16 [4096, 14336], P(None, 'tp'), may hold values from -0.09375 to 0.09375
- up_matrix: bfloat16 [4096, 14336], P(None, 'tp'), may hold values from -0.09375 to 0.09375
- down_matrix: bfloat16 [14336, 4096], P('tp'), may hold values from -0.046875 to 0.046875
- adapter_gate_up_inputs: bfloat16 [64, 4096, 128], P('grp', 'tp'), may hold values from -0.09375 to 0.09375
- adapter_gate_up_outputs: bfloat16 [64, 128, 14336], P('grp', None, 'tp'), may hold values from -0.75 to 0.75
- adapter_down_inputs: bfloat16 [64, 14336, 64], P('grp', 'tp'), may hold values from -0.046875 to 0.046875
- adapter_down_outputs: bfloat16 [64, 64, 4096], P('grp', None, 'tp'), may hold values from -0.75 to 0.75
Outputs:
- mixed: bfloat16 [2048, 4096], P('grp', 'tp')
The draws below stay inside these ranges and needn't reach their ends.
Inputs may be any that keep to these rules, and one draw needn't show every extreme that they name: `token_tenant`: within each aligned block of 512 tokens, at most 256 tokens have tenants whose slot lies in one storage block of 16 slots; one storage block, chosen from the seed, receives exactly 256 tokens from every such block. `tenant_storage_slot`: A permutation of the tenants.
All inputs are finite; a program needn't handle non-finite values.
Results may differ from the reference program's by a relative error of at most 0.017.
Values may be sent and summed in bfloat16 or wider, within the bound.
A program may use at most 128 MiB of HBM per device.

```python
import jax
import jax.numpy as jnp
from jax import lax

MODEL_WIDTH = 4096
HIDDEN_UNITS = 14336
ADAPTER_RANK = 64
TENANT_COUNT = 64
TOK_G = 512
TOKENS = 2048
TENANTS_PER_BLOCK = 16
CAP = 256
N_GRP = 4


def routing(key):
    home = jax.random.permutation(jax.random.fold_in(key, 11), TENANT_COUNT).astype(jnp.int32)
    hot = jax.random.randint(jax.random.fold_in(key, 12), (), 0, N_GRP).astype(jnp.int32)
    group_keys = jax.random.split(jax.random.fold_in(key, 13), N_GRP)

    def one_group(group_key):
        first_key, second_key = jax.random.split(group_key)
        ranks = jax.random.permutation(first_key, TOK_G).astype(jnp.int32)
        spread = (ranks - CAP) % (N_GRP - 1)
        other = spread + (spread >= hot).astype(jnp.int32)
        server = jnp.where(ranks < CAP, hot, other)
        local = jax.random.randint(second_key, (TOK_G,), 0, TENANTS_PER_BLOCK).astype(jnp.int32)
        return server * TENANTS_PER_BLOCK + local
    slots = jax.vmap(one_group)(group_keys).reshape(-1)
    owner = jnp.argsort(home).astype(jnp.int32)
    tenant = owner[slots].astype(jnp.int32)
    return (tenant, home)


def draw_token_tenant(key, part):
    return routing(key)[0]


def draw_tenant_storage_slot(key, part):
    return routing(key)[1]


def steps_of(rng, extent, shards, low, high):
    gain, own = 1.0, jax.random.fold_in(rng, 6)
    for dim, shards_of in shards:
        draws = jnp.exp(jax.random.uniform(jax.random.fold_in(own, dim), (shards_of,), jnp.float32, low / len(shards), high / len(shards)))
        gain = gain * jnp.repeat(draws, extent[dim] // shards_of).reshape([-1 if axis == dim else 1 for axis in range(len(extent))])
    return gain


def bell_draw(stream_key, shape, scale, reach, shards=(), kind=jnp.bfloat16):
    values = jax.random.normal(stream_key, shape, jnp.float32) * scale
    if len(shards) > 0:
        values = steps_of(stream_key, shape, shards, -0.22, 0.18) * values
    return jnp.clip(values, min=-reach, max=reach).astype(kind)


def setup_inputs(seed: int = 0) -> dict:
    splits = jax.random.split(jax.random.key(seed), 11)
    return {
        "tokens": bell_draw(splits[0], (TOKENS, MODEL_WIDTH), 1.0, 6.0, ((0, 4), (1, 8))),
        "token_tenant": draw_token_tenant(jax.random.fold_in(splits[10], 71), 0),
        "tenant_storage_slot": draw_tenant_storage_slot(jax.random.fold_in(splits[10], 71), 0),
        "gate_matrix": bell_draw(splits[3], (MODEL_WIDTH, HIDDEN_UNITS), MODEL_WIDTH ** -0.5, 0.09375, ((1, 8),)),
        "up_matrix": bell_draw(splits[4], (MODEL_WIDTH, HIDDEN_UNITS), MODEL_WIDTH ** -0.5, 0.09375, ((1, 8),)),
        "down_matrix": bell_draw(splits[5], (HIDDEN_UNITS, MODEL_WIDTH), HIDDEN_UNITS ** -0.5, 0.046875, ((0, 8),)),
        "adapter_gate_up_inputs": bell_draw(splits[6], (TENANT_COUNT, MODEL_WIDTH, 2 * ADAPTER_RANK), MODEL_WIDTH ** -0.5, 0.09375, ((0, 4), (1, 8))),
        "adapter_gate_up_outputs": bell_draw(splits[7], (TENANT_COUNT, 2 * ADAPTER_RANK, HIDDEN_UNITS), ADAPTER_RANK ** -0.5, 0.75, ((0, 4), (2, 8))),
        "adapter_down_inputs": bell_draw(splits[8], (TENANT_COUNT, HIDDEN_UNITS, ADAPTER_RANK), HIDDEN_UNITS ** -0.5, 0.046875, ((0, 4), (1, 8))),
        "adapter_down_outputs": bell_draw(splits[9], (TENANT_COUNT, ADAPTER_RANK, MODEL_WIDTH), ADAPTER_RANK ** -0.5, 0.75, ((0, 4), (2, 8))),
    }


def expand(onehot, vec):
    wide = onehot[:, :, None] * vec.astype(jnp.float32)[:, None, :]
    return wide.reshape(vec.shape[0], -1).astype(jnp.bfloat16)


def reference(tokens, token_tenant, tenant_storage_slot, gate_matrix, up_matrix, down_matrix, adapter_gate_up_inputs, adapter_gate_up_outputs, adapter_down_inputs, adapter_down_outputs):
    slot = tenant_storage_slot[token_tenant].astype(jnp.int32)
    server = slot // TENANTS_PER_BLOCK
    local = slot - server * TENANTS_PER_BLOCK
    width = N_GRP * CAP
    order = jnp.argsort(server, stable=True).astype(jnp.int32)
    counts = jnp.sum((server[:, None] == jnp.arange(N_GRP, dtype=jnp.int32)[None, :]).astype(jnp.int32), 0)
    starts = (jnp.cumsum(counts) - counts).astype(jnp.int32)
    padded = jnp.concatenate([order, jnp.zeros((width,), jnp.int32)])
    lanes = jnp.arange(TENANTS_PER_BLOCK, dtype=jnp.int32)

    def select(storage_block):
        picked = lax.dynamic_slice(padded, (starts[storage_block],), (width,))
        live = jnp.arange(width, dtype=jnp.int32) < counts[storage_block]
        onehot = jnp.where(live[:, None] & (local[picked][:, None] == lanes[None, :]), 1.0, 0.0).astype(jnp.float32)
        return picked, live, onehot

    def gate_up_step(carry, storage_block):
        total_gate, total_up = carry
        picked, live, onehot = select(storage_block)
        input_factor = lax.dynamic_slice_in_dim(adapter_gate_up_inputs, storage_block * TENANTS_PER_BLOCK, TENANTS_PER_BLOCK, 0)
        output_factor = lax.dynamic_slice_in_dim(adapter_gate_up_outputs, storage_block * TENANTS_PER_BLOCK, TENANTS_PER_BLOCK, 0)
        rows = tokens[picked].astype(jnp.float32)
        part = jnp.einsum('ny,eyq->neq', rows, input_factor.astype(jnp.float32))
        ranks = jnp.sum(part * onehot[:, :, None], 1).astype(jnp.bfloat16)
        gate_output_factor = output_factor[:, :ADAPTER_RANK, :].reshape(TENANTS_PER_BLOCK * ADAPTER_RANK, HIDDEN_UNITS)
        up_output_factor = output_factor[:, ADAPTER_RANK:, :].reshape(TENANTS_PER_BLOCK * ADAPTER_RANK, HIDDEN_UNITS)
        delta_gate = jnp.dot(expand(onehot, ranks[:, :ADAPTER_RANK]), gate_output_factor, preferred_element_type=jnp.float32).astype(jnp.bfloat16)
        delta_up = jnp.dot(expand(onehot, ranks[:, ADAPTER_RANK:]), up_output_factor, preferred_element_type=jnp.float32).astype(jnp.bfloat16)
        zero = jnp.zeros((), jnp.bfloat16)
        total_gate = total_gate.at[picked].add(jnp.where(live[:, None], delta_gate, zero))
        total_up = total_up.at[picked].add(jnp.where(live[:, None], delta_up, zero))
        return (total_gate, total_up), None

    empty = jnp.zeros((TOKENS, HIDDEN_UNITS), jnp.bfloat16)
    blocks = jnp.arange(N_GRP, dtype=jnp.int32)
    (delta_gate, delta_up), _ = lax.scan(gate_up_step, (empty, empty), blocks)
    gate = jnp.dot(tokens, gate_matrix, preferred_element_type=jnp.float32) + delta_gate.astype(jnp.float32)
    up = jnp.dot(tokens, up_matrix, preferred_element_type=jnp.float32) + delta_up.astype(jnp.float32)
    hidden = (jax.nn.silu(gate) * up).astype(jnp.bfloat16)

    def down_step(total, storage_block):
        picked, live, onehot = select(storage_block)
        input_factor = lax.dynamic_slice_in_dim(adapter_down_inputs, storage_block * TENANTS_PER_BLOCK, TENANTS_PER_BLOCK, 0)
        output_factor = lax.dynamic_slice_in_dim(adapter_down_outputs, storage_block * TENANTS_PER_BLOCK, TENANTS_PER_BLOCK, 0)
        rows = hidden[picked].astype(jnp.float32)
        part = jnp.einsum('us,ysc->uyc', rows, input_factor.astype(jnp.float32))
        ranks = jnp.sum(part * onehot[:, :, None], 1).astype(jnp.bfloat16)
        delta = jnp.dot(expand(onehot, ranks), output_factor.reshape(TENANTS_PER_BLOCK * ADAPTER_RANK, MODEL_WIDTH), preferred_element_type=jnp.float32).astype(jnp.bfloat16)
        total = total.at[picked].add(jnp.where(live[:, None], delta, jnp.zeros((), jnp.bfloat16)))
        return total, None

    delta_down, _ = lax.scan(down_step, jnp.zeros((TOKENS, MODEL_WIDTH), jnp.bfloat16), blocks)
    mixed = jnp.dot(hidden, down_matrix, preferred_element_type=jnp.float32) + delta_down.astype(jnp.float32)
    return mixed.astype(jnp.bfloat16)
```

```python
import jax
import jax.numpy as jnp
from jax import lax
from jax.sharding import PartitionSpec as P

F32 = jnp.float32
BF16 = jnp.bfloat16


def slots_of(tenant, storage_slot):
    table = jnp.arange(storage_slot.shape[0], dtype=jnp.int32)
    match = tenant[..., None] == table
    return jnp.sum(jnp.where(match, storage_slot, 0), -1)


def spread_onehot(onehot, vec):
    wide = onehot[:, :, None] * vec[:, None, :]
    return wide.reshape(vec.shape[0], -1)


def dot(a, b):
    return jnp.dot(a, b, preferred_element_type=F32)


def body(
    tokens,
    token_tenant,
    tenant_storage_slot,
    gate_matrix,
    up_matrix,
    down_matrix,
    adapter_gate_up_inputs,
    adapter_gate_up_outputs,
    adapter_down_inputs,
    adapter_down_outputs,
):
    groups = lax.axis_size("grp")
    me = lax.axis_index("grp")
    rows = tokens.shape[0]
    block_slots = adapter_gate_up_inputs.shape[0]
    rank = adapter_gate_up_inputs.shape[2] // 2
    hidden_share = gate_matrix.shape[1]
    width_share = tokens.shape[1]
    capacity = 2 * rows // groups

    slot = slots_of(token_tenant, tenant_storage_slot)
    server = slot // block_slots
    order = jnp.arange(rows, dtype=jnp.int32)
    upto = (order[:, None] >= order[None, :]).astype(BF16)
    picks = (server[:, None] == jnp.arange(groups, dtype=jnp.int32)[None, :]).astype(BF16)
    count = dot(upto, picks)
    place = jnp.sum(picks.astype(F32) * (count - 1.0), 1).astype(jnp.int32)
    target = server * capacity + place
    seat = jnp.arange(groups * capacity, dtype=jnp.int32)
    pack = (seat[:, None] == target[None, :]).astype(BF16)
    sent = dot(pack, tokens).astype(BF16).reshape(groups, capacity, width_share)
    got = lax.all_to_all(sent, "grp", split_axis=0, concat_axis=0, tiled=True)
    got = got.reshape(groups * capacity, width_share)
    piece = lax.all_gather(got, "tp", axis=1, tiled=True)

    all_tenant = lax.all_gather(token_tenant, "grp", axis=0)
    all_slot = slots_of(all_tenant, tenant_storage_slot)
    here = all_slot // block_slots == me
    local = all_slot - me * block_slots
    all_place = dot(here.astype(BF16), upto.T).astype(jnp.int32) - 1
    all_place = jnp.where(here, all_place, -1)
    seats = (
        jnp.arange(capacity, dtype=jnp.int32)[None, :, None] == all_place[:, None, :]
    ).astype(BF16)
    lanes = (local[:, :, None] == jnp.arange(block_slots, dtype=jnp.int32)).astype(BF16)
    onehot = jnp.einsum("gcr,gre->gce", seats, lanes, preferred_element_type=F32)
    onehot = onehot.astype(BF16).reshape(groups * capacity, block_slots)
    onehot_wide = onehot.astype(F32)[:, :, None]

    part = jnp.einsum("ny,eyq->neq", got, adapter_gate_up_inputs, preferred_element_type=F32)
    part = jnp.sum(part * onehot_wide, 1)
    ranks = lax.psum(part, "tp").astype(BF16)
    gate_factor = adapter_gate_up_outputs[:, :rank, :].reshape(block_slots * rank, hidden_share)
    up_factor = adapter_gate_up_outputs[:, rank:, :].reshape(block_slots * rank, hidden_share)
    delta_gate = dot(spread_onehot(onehot, ranks[:, :rank]), gate_factor).astype(BF16)
    delta_up = dot(spread_onehot(onehot, ranks[:, rank:]), up_factor).astype(BF16)

    gate = dot(piece, gate_matrix) + delta_gate.astype(F32)
    up = dot(piece, up_matrix) + delta_up.astype(F32)
    hidden = (jax.nn.silu(gate) * up).astype(BF16)

    down_part = jnp.einsum("us,ysc->uyc", hidden, adapter_down_inputs, preferred_element_type=F32)
    down_part = jnp.sum(down_part * onehot_wide, 1)
    down_ranks = lax.psum(down_part.astype(BF16), "tp")
    down_factor = adapter_down_outputs.reshape(block_slots * rank, width_share)
    delta_down = dot(spread_onehot(onehot, down_ranks), down_factor).astype(BF16)
    base = lax.psum_scatter(
        dot(hidden, down_matrix).astype(BF16), "tp", scatter_dimension=1, tiled=True
    )
    mixed = (base.astype(F32) + delta_down.astype(F32)).astype(BF16)
    back = lax.all_to_all(
        mixed.reshape(groups, capacity, width_share),
        "grp",
        split_axis=0,
        concat_axis=0,
        tiled=True,
    ).reshape(groups * capacity, width_share)
    unpack = (target[:, None] == seat[None, :]).astype(BF16)
    return dot(unpack, back).astype(BF16)


def solution(mesh):
    return jax.shard_map(
        body,
        mesh=mesh,
        in_specs=(
            P("grp", "tp"),
            P("grp"),
            P(),
            P(None, "tp"),
            P(None, "tp"),
            P("tp", None),
            P("grp", "tp", None),
            P("grp", None, "tp"),
            P("grp", "tp", None),
            P("grp", None, "tp"),
        ),
        out_specs=P("grp", "tp"),
        check_vma=False,
    )
```
